128 devices in a mesh: row: 8 (over x, z_hi), col: 16 (over y, z_lo, core).
Axes of the slice: x: 4, y: 4, z: 4 (z_hi: 2, z_lo: 2; z = z_hi * 2 + z_lo), core: 2. Of those that a mesh axis runs over, the one named last changes fastest.
Arguments:
- increments: bfloat16 [2048, 8192], P('col', 'row'), may hold values from -48 to 48
- states: bfloat16 [2048, 65536], P(('row', 'col')), may hold values from -24 to 24
- group_date: int32 [128], replicated, may hold values from 0 to 127, each once
Outputs:
- covariance: float32 [8192, 65536], P('row', 'col')
The draws below stay inside these ranges and needn't reach their ends.
Inputs may be any that keep to these rules, and one draw needn't show every extreme that they name: `group_date`: a permutation: each of the 128 date groups is named once.
All inputs are finite; a program needn't handle non-finite values.
Results may differ from the reference program's by a relative error of at most 0.0003.
Values may be sent and summed in bfloat16 or wider, within the bound.
No kernel may reach another device: no remote copies, remote signals or barrier semaphores. Data moves between devices by JAX's collectives and lax.ppermute only.
A program may use at most 128 MiB of HBM per device.

```python
import jax
import jax.numpy as jnp

R = 8192
S = 65536
TC = 16
NCHUNK = 128
DATES = 2048


def spiked(drawn, rng, source, target, shards_of, factor):
    owner, partner = [(jnp.arange(drawn.shape[position]) // (drawn.shape[position] // shards_of)).reshape([-1 if axis == position else 1 for axis in range(drawn.ndim)]) for position in (source, target)]
    chosen = jax.random.permutation(rng, shards_of)[partner]
    strong = (owner == chosen) | (owner == (partner + shards_of // 2) % shards_of)
    return jnp.where(strong, factor * drawn, drawn)


def steps_of(stream_key, extent, cuts, least, largest):
    factor_of, own = 1.0, jax.random.fold_in(stream_key, 6)
    for dim, parts in cuts:
        steps = jnp.exp(jax.random.uniform(jax.random.fold_in(own, dim), (parts,), jnp.float32, least / len(cuts), largest / len(cuts)))
        factor_of = factor_of * jnp.repeat(steps, extent[dim] // parts).reshape([-1 if axis == dim else 1 for axis in range(len(extent))])
    return factor_of


def scatter_about(key, shape, width, reach, pieces=(), held_as=jnp.bfloat16):
    factor_of = steps_of(key, shape, pieces, -0.22, 0.18) if pieces else 1.0
    entries = jax.random.normal(key, shape, jnp.float32) * width * factor_of
    return jnp.minimum(jnp.maximum(entries, -reach), reach).astype(held_as)


def heavy_noise(own_key, dims, deviation, limit, shards, heavy, held_as=jnp.bfloat16):
    result = deviation * jax.random.normal(own_key, dims, jnp.float32)
    if shards:
        result = result * steps_of(own_key, dims, shards, -0.22, 0.18)
    return jnp.clip(spiked(result, jax.random.fold_in(own_key, 3), *heavy), -limit, limit).astype(held_as)


def setup_inputs(seed: int = 0) -> dict:
    key_of = jax.random.split(jax.random.key(seed), 4)
    increments = scatter_about(key_of[0], (DATES, R), 8.0, 48.0, ((0, 16), (1, 8)))
    states = heavy_noise(key_of[1], (DATES, S), 1.0, 24.0, ((0, 128),), (0, 1, 128, 5.5))
    group_date = jax.random.permutation(key_of[2], NCHUNK).astype(jnp.int32)
    return dict(increments=increments, states=states, group_date=group_date)


def reference(increments, states, group_date):
    aligned = increments.reshape(NCHUNK, TC, R)[group_date].reshape(DATES, R)
    inc_mean = jnp.sum(increments.astype(jnp.float32), axis=0) / DATES
    state_mean = jnp.sum(states.astype(jnp.float32), axis=0) / DATES
    cross = jnp.dot(aligned.T, states, preferred_element_type=jnp.float32)
    correction = DATES * (inc_mean[:, None] * state_mean[None, :])
    return (cross - correction) / (DATES - 1)
```

```python
import functools

import jax
import jax.numpy as jnp
from jax import lax
from jax.experimental import pallas as pl
from jax.experimental.pallas import tpu as pltpu
from jax.sharding import PartitionSpec as P

AXES = ("row", "col")
NX, NY, NZ, NC = 4, 4, 4, 2
NCOL = NY * 2 * NC
TILE = 512
WIDTHS = (1024, 1536, 1536)


def device(x, y, z, c):
    return ((x % NX) * 2 + (z % NZ) // 2) * NCOL + ((y % NY) * 2 + (z % NZ) % 2) * NC + c


def moves(to):
    return [
        (device(x, y, z, c), device(*to(x, y, z, c)))
        for x in range(NX) for y in range(NY) for z in range(NZ) for c in range(NC)
    ]


X_UP = moves(lambda x, y, z, c: (x + 1, y, z, c))
X_DOWN = moves(lambda x, y, z, c: (x - 1, y, z, c))
X_FAR = moves(lambda x, y, z, c: (x + 2, y, z, c))
SAME_X = [[x * 2 * NCOL + i for i in range(2 * NCOL)] for x in range(NX)]
ALONG_X = [[2 * x + h for x in range(NX)] for h in range(2)]


def align_kernel(starts, inc_ref, out_ref, sum_ref, held, sem):
    dates, comps = held.shape
    group = dates // starts.shape[0]

    def send(i, carry):
        source = pl.multiple_of(starts[i], group)
        target = pl.multiple_of(i * group, group)
        pltpu.make_async_copy(
            inc_ref.at[pl.ds(source, group)], held.at[pl.ds(target, group)], sem
        ).start()
        return carry

    lax.fori_loop(0, starts.shape[0], send, 0)
    pltpu.make_async_copy(inc_ref, held, sem).wait()
    step = 256
    total = jnp.zeros((comps, 1), jnp.float32)
    for i in range(dates // step):
        turned = held[i * step:(i + 1) * step, :].T
        out_ref[:, i * step:(i + 1) * step] = turned
        total = total + jnp.sum(turned.astype(jnp.float32), axis=1, keepdims=True)
    sum_ref[...] = total


def align(starts, inc_all):
    dates, comps = inc_all.shape
    return pl.pallas_call(
        align_kernel,
        out_shape=(
            jax.ShapeDtypeStruct((comps, dates), inc_all.dtype),
            jax.ShapeDtypeStruct((comps, 1), jnp.float32),
        ),
        in_specs=[
            pl.BlockSpec(memory_space=pltpu.SMEM),
            pl.BlockSpec(memory_space=pl.ANY),
        ],
        out_specs=(
            pl.BlockSpec(memory_space=pltpu.VMEM),
            pl.BlockSpec(memory_space=pltpu.VMEM),
        ),
        scratch_shapes=[pltpu.VMEM((dates, comps), inc_all.dtype), pltpu.SemaphoreType.DMA],
        compiler_params=pltpu.CompilerParams(vmem_limit_bytes=60 * 2**20),
        cost_estimate=pl.CostEstimate(flops=comps, bytes_accessed=comps, transcendentals=0),
        name="align",
    )(starts, inc_all)


def gather_panel(places, panels):
    return [(0, panels[0][...])]


def exchange_panel(places, panels):
    sources, nx, group, width = panels[0].shape
    depth = sources * group
    return [
        (pl.multiple_of(places[i], depth), panels[0][:, i].reshape(depth, width))
        for i in range(nx)
    ]


def ring_panel(places, panels):
    order = (0, 1, 3, 2, 4)
    return [
        (pl.multiple_of(places[i], panel.shape[0]), panel[...]) for i, panel in zip(order, panels)
    ]


def product_kernel(pieces, places, rows_ref, sum_ref, *refs):
    dates = rows_ref.shape[1]
    panels, out_ref = refs[:-1], refs[-1]
    acc, state_sum = None, None
    for place, piece in pieces(places, panels):
        part = jnp.dot(
            rows_ref[:, pl.ds(place, piece.shape[0])], piece, preferred_element_type=jnp.float32
        )
        partial_sum = jnp.sum(piece.astype(jnp.float32), axis=0, keepdims=True)
        acc = part if acc is None else acc + part
        state_sum = partial_sum if state_sum is None else state_sum + partial_sum
    inc_mean = sum_ref[...] / dates
    state_mean = state_sum / dates
    out_ref[...] = (acc - dates * (inc_mean * state_mean)) * (1.0 / (dates - 1))


def product(pieces, places, rows, inc_sum, panels, offset, columns, out):
    comps, dates = rows.shape
    width = panels[0].shape[-1]
    base = offset // TILE
    whole = pl.Buffered(1)
    in_specs = [
        pl.BlockSpec(memory_space=pltpu.SMEM),
        pl.BlockSpec(rows.shape, lambda j: (0, 0), pipeline_mode=whole),
        pl.BlockSpec(inc_sum.shape, lambda j: (0, 0), pipeline_mode=whole),
    ]
    for panel in panels:
        lead = (0,) * (panel.ndim - 1)
        in_specs.append(pl.BlockSpec(panel.shape[:-1] + (TILE,), lambda j, lead=lead: lead + (j,)))
    args = [places, rows, inc_sum] + panels
    aliases = {}
    kernel = functools.partial(product_kernel, pieces)
    if out is not None:
        in_specs.append(pl.BlockSpec(memory_space=pl.ANY))
        aliases = {len(args): 0}
        args.append(out)

        def kernel(*refs):
            product_kernel(pieces, *refs[:-2], refs[-1])

    return pl.pallas_call(
        kernel,
        out_shape=jax.ShapeDtypeStruct((comps, columns), jnp.float32),
        grid=(width // TILE,),
        in_specs=in_specs,
        out_specs=pl.BlockSpec((comps, TILE), lambda j: (0, base + j)),
        input_output_aliases=aliases,
        compiler_params=pltpu.CompilerParams(vmem_limit_bytes=60 * 2**20),
        cost_estimate=pl.CostEstimate(flops=comps, bytes_accessed=comps, transcendentals=0),
        name="product",
    )(*args)


def body(increments, states, group_date):
    group, total = states.shape
    columns = total // NCOL
    dates = group * group_date.shape[0]
    blocks = states.reshape(group, NCOL, columns)
    barrier = lax.optimization_barrier

    def part(offset, width):
        return blocks[:, :, offset:offset + width].transpose(1, 0, 2)

    def spread(got):
        return lax.all_gather(got, "row", axis=0, tiled=True, axis_index_groups=ALONG_X)

    def exchange(sent):
        both = jnp.broadcast_to(sent[None], (2,) + sent.shape).reshape((-1,) + sent.shape[1:])
        return lax.all_to_all(both, AXES, 0, 0, tiled=True, axis_index_groups=SAME_X)

    wa, wb, wc = WIDTHS
    x = lax.axis_index("row") // 2
    depth = dates // NX
    places = jnp.stack(
        [(x + step) % NX * depth for step in range(NX)] + [(x + 2) % NX * depth + depth // 2]
    ).astype(jnp.int32)

    inc_all = lax.all_gather(increments, "col", axis=0, tiled=True)
    raw = part(0, wa)
    raw_left = lax.ppermute(raw, AXES, X_UP)
    raw_right = lax.ppermute(raw, AXES, X_DOWN)
    raw_far = lax.ppermute(raw, AXES, X_FAR)
    gotc = exchange(part(wa + wb, wc)).reshape(-1, wc)

    sentb, raw, raw_left, raw_right, raw_far, gotc = barrier(
        (part(wa, wb), raw, raw_left, raw_right, raw_far, gotc)
    )
    left = lax.ppermute(gotc, AXES, X_UP)
    right = lax.ppermute(gotc, AXES, X_DOWN)
    gotb = exchange(sentb).reshape(-1, wb)

    raw, raw_left, raw_right, raw_far, gotc, left, right, gotb = barrier(
        (raw, raw_left, raw_right, raw_far, gotc, left, right, gotb)
    )
    panelb = spread(gotb)
    far_left = lax.ppermute(left[:depth // 2], AXES, X_UP)
    far_right = lax.ppermute(right[depth // 2:], AXES, X_DOWN)
    raw = jnp.stack([raw, raw_right, raw_far, raw_left], axis=1)
    gota = exchange(raw.reshape(NCOL, NX * group, wa)).reshape(2 * NCOL, NX, group, wa)
    rows, inc_sum = align(group_date * group, inc_all)
    ring = [gotc, right, left, far_left, far_right]
    out = product(ring_panel, places, rows, inc_sum, ring, wa + wb, columns, None)

    gota, out = barrier((gota, out))
    out = product(exchange_panel, places, rows, inc_sum, [gota], 0, columns, out)
    return product(gather_panel, places, rows, inc_sum, [panelb], wa, columns, out)


def solution(mesh):
    in_specs = (P("col", "row"), P(("row", "col"), None), P())
    out_specs = P("row", "col")
    return jax.shard_map(body, mesh=mesh, in_specs=in_specs, out_specs=out_specs, check_vma=False)
```

```python
import functools

import jax
import jax.numpy as jnp
from jax import lax
from jax.experimental import pallas as pl
from jax.experimental.pallas import tpu as pltpu
from jax.sharding import PartitionSpec as P

AXES = ("row", "col")
NX, NY, NZ, NC = 4, 4, 4, 2
NCOL = NY * 2 * NC
TILE = 512
BLOCK = 256
WEIGHT = 8
WIDTHS = (1024, 1536, 1536)


def device(x, y, z, c):
    return ((x % NX) * 2 + (z % NZ) // 2) * NCOL + ((y % NY) * 2 + (z % NZ) % 2) * NC + c


def moves(to):
    return [
        (device(x, y, z, c), device(*to(x, y, z, c)))
        for x in range(NX) for y in range(NY) for z in range(NZ) for c in range(NC)
    ]


X_UP = moves(lambda x, y, z, c: (x + 1, y, z, c))
X_DOWN = moves(lambda x, y, z, c: (x - 1, y, z, c))
X_FAR = moves(lambda x, y, z, c: (x + 2, y, z, c))
Y_UP = moves(lambda x, y, z, c: (x, y + 1, z, c))
Y_DOWN = moves(lambda x, y, z, c: (x, y - 1, z, c))
Y_FAR = moves(lambda x, y, z, c: (x, y + 2, z, c))
Z_PAIR = moves(lambda x, y, z, c: (x, y, z ^ 1, c))
CORE = moves(lambda x, y, z, c: (x, y, z, 1 - c))
SAME_X = [[x * 2 * NCOL + i for i in range(2 * NCOL)] for x in range(NX)]


def copy_all(copies, sems):
    started = [pltpu.make_async_copy(a, b, sems.at[i]) for i, (a, b) in enumerate(copies)]
    for copy in started:
        copy.start()
    for copy in started:
        copy.wait()


def repeat(held, out_ref, sems):
    targets = held.shape[0]
    times = out_ref.shape[0] // targets
    copy_all([(held, out_ref.at[pl.ds(i * targets, targets)]) for i in range(times)], sems)


def pick_kernel(offset, states_ref, out_ref, held, sems):
    targets, _, width = held.shape
    columns = states_ref.shape[1] // targets
    copy_all(
        [
            (states_ref.at[:, pl.ds(t * columns + offset, width)], held.at[t])
            for t in range(targets)
        ],
        sems,
    )
    repeat(held, out_ref, sems)


def pick(states, offset, width, times):
    shape = (NCOL, states.shape[0], width)
    return pl.pallas_call(
        functools.partial(pick_kernel, offset),
        out_shape=jax.ShapeDtypeStruct((times * NCOL,) + shape[1:], states.dtype),
        in_specs=[pl.BlockSpec(memory_space=pl.ANY)],
        out_specs=pl.BlockSpec(memory_space=pl.ANY),
        scratch_shapes=[pltpu.VMEM(shape, states.dtype), pltpu.SemaphoreType.DMA((NCOL,))],
        compiler_params=pltpu.CompilerParams(vmem_limit_bytes=60 * 2**20),
        cost_estimate=pl.CostEstimate(flops=width, bytes_accessed=width, transcendentals=0),
        name="pick",
    )(states)


def join_kernel(*refs):
    parts, out_ref, held, sems = refs[:-3], refs[-3], refs[-2], refs[-1]
    copy_all([(part, held.at[:, i]) for i, part in enumerate(parts)], sems)
    repeat(held, out_ref, sems)


def join(parts):
    targets, group, width = parts[0].shape
    shape = (targets, len(parts), group, width)
    return pl.pallas_call(
        join_kernel,
        out_shape=jax.ShapeDtypeStruct((2 * targets,) + shape[1:], parts[0].dtype),
        in_specs=[pl.BlockSpec(memory_space=pl.ANY)] * len(parts),
        out_specs=pl.BlockSpec(memory_space=pl.ANY),
        scratch_shapes=[
            pltpu.VMEM(shape, parts[0].dtype),
            pltpu.SemaphoreType.DMA((len(parts),)),
        ],
        compiler_params=pltpu.CompilerParams(vmem_limit_bytes=60 * 2**20),
        cost_estimate=pl.CostEstimate(flops=width, bytes_accessed=width, transcendentals=0),
        name="join",
    )(*parts)


def align_kernel(starts, mine_ref, other_ref, out_ref, sum_ref, held, sem):
    dates, comps = held.shape
    group = dates // starts.shape[0]
    half = dates // 2

    def send(i, carry):
        start = starts[i]
        target = held.at[pl.ds(pl.multiple_of(i * group, group), group)]

        @pl.when(start < half)
        def _():
            source = mine_ref.at[pl.ds(pl.multiple_of(start, group), group)]
            pltpu.make_async_copy(source, target, sem).start()

        @pl.when(start >= half)
        def _():
            source = other_ref.at[pl.ds(pl.multiple_of(start - half, group), group)]
            pltpu.make_async_copy(source, target, sem).start()

        return carry

    lax.fori_loop(0, starts.shape[0], send, 0)
    pltpu.make_async_copy(held, held, sem).wait()
    step = 256
    total = jnp.zeros((comps, 1), jnp.float32)
    for i in range(dates // step):
        turned = held[i * step:(i + 1) * step, :].T
        out_ref[:, i * step:(i + 1) * step] = turned
        total = total + jnp.sum(turned.astype(jnp.float32), axis=1, keepdims=True)
    sum_ref[...] = total


def align(starts, mine, other):
    dates, comps = 2 * mine.shape[0], mine.shape[1]
    return pl.pallas_call(
        align_kernel,
        out_shape=(
            jax.ShapeDtypeStruct((comps, dates), mine.dtype),
            jax.ShapeDtypeStruct((comps, 1), jnp.float32),
        ),
        in_specs=[
            pl.BlockSpec(memory_space=pltpu.SMEM),
            pl.BlockSpec(memory_space=pl.ANY),
            pl.BlockSpec(memory_space=pl.ANY),
        ],
        out_specs=(
            pl.BlockSpec(memory_space=pltpu.VMEM),
            pl.BlockSpec(memory_space=pltpu.VMEM),
        ),
        scratch_shapes=[pltpu.VMEM((dates, comps), mine.dtype), pltpu.SemaphoreType.DMA],
        compiler_params=pltpu.CompilerParams(vmem_limit_bytes=60 * 2**20),
        cost_estimate=pl.CostEstimate(flops=comps, bytes_accessed=comps, transcendentals=0),
        name="align",
    )(starts, mine, other)


def exchange_panel(places, panels):
    sources, nx, group, width = panels[0].shape
    depth = sources * group
    return [
        (pl.multiple_of(places[i], depth), panels[0][:, i].reshape(depth, width))
        for i in range(nx)
    ]


def ring_panel(places, panels):
    order = (0, 1, 3, 2, 4)
    return [
        (pl.multiple_of(places[i], panel.shape[0]), panel[...]) for i, panel in zip(order, panels)
    ]


def product_kernel(pieces, places, rows_ref, sum_ref, *refs):
    comps, dates = rows_ref.shape
    panels, out_ref = refs[:-1], refs[-1]
    parts = pieces(places, panels)
    state_sum = sum(jnp.sum(part.astype(jnp.float32), axis=0, keepdims=True) for _, part in parts)
    state_mean = state_sum / dates
    for start in range(0, comps, BLOCK):
        block = pl.ds(start, BLOCK)
        acc = sum(
            jnp.dot(
                rows_ref[block, pl.ds(place, part.shape[0])],
                part,
                preferred_element_type=jnp.float32,
            )
            for place, part in parts
        )
        inc_mean = sum_ref[block, :] / dates
        out_ref[block, :] = (acc - dates * (inc_mean * state_mean)) * (1.0 / (dates - 1))


def product(pieces, places, rows, inc_sum, panels, offset, columns, out):
    comps, dates = rows.shape
    width = panels[0].shape[-1]
    tile = TILE if width % TILE == 0 and offset % TILE == 0 else TILE // 2
    base = offset // tile
    whole = pl.Buffered(1)
    in_specs = [
        pl.BlockSpec(memory_space=pltpu.SMEM),
        pl.BlockSpec(rows.shape, lambda j: (0, 0), pipeline_mode=whole),
        pl.BlockSpec(inc_sum.shape, lambda j: (0, 0), pipeline_mode=whole),
    ]
    for panel in panels:
        lead = (0,) * (panel.ndim - 1)
        in_specs.append(pl.BlockSpec(panel.shape[:-1] + (tile,), lambda j, lead=lead: lead + (j,)))
    args = [places, rows, inc_sum] + panels
    aliases = {}
    kernel = functools.partial(product_kernel, pieces)
    if out is not None:
        in_specs.append(pl.BlockSpec(memory_space=pl.ANY))
        aliases = {len(args): 0}
        args.append(out)

        def kernel(*refs):
            product_kernel(pieces, *refs[:-2], refs[-1])

    return pl.pallas_call(
        kernel,
        out_shape=jax.ShapeDtypeStruct((comps, columns), jnp.float32),
        grid=(width // tile,),
        in_specs=in_specs,
        out_specs=pl.BlockSpec((comps, tile), lambda j: (0, base + j)),
        input_output_aliases=aliases,
        compiler_params=pltpu.CompilerParams(vmem_limit_bytes=60 * 2**20),
        cost_estimate=pl.CostEstimate(
            flops=2 * comps * dates * width * WEIGHT,
            bytes_accessed=(2 * comps * dates + 2 * dates * width + 4 * comps * width) * WEIGHT,
            transcendentals=0,
        ),
        name="product",
    )(*args)


def group_places(group_date, group):
    per = group_date.shape[0] // NCOL
    col = lax.axis_index("col")
    y, zl, c = col // (2 * NC), (col // NC) % 2, col % NC
    owner = group_date // per
    oy, oz, oc = owner // (2 * NC), (owner // NC) % 2, owner % NC
    place = ((((oc + c) % 2) * NY + (oy - y + NY) % NY) * 2 + (oz + zl) % 2) * per + group_date % per
    return (place * group).astype(jnp.int32)


def body(increments, states, group_date):
    group, total = states.shape
    columns = total // NCOL
    dates = group * group_date.shape[0]
    barrier = lax.optimization_barrier

    def exchange(sent):
        return lax.all_to_all(sent, AXES, 0, 0, tiled=True, axis_index_groups=SAME_X)

    wa, wb, wc = WIDTHS
    x = lax.axis_index("row") // 2
    depth = dates // NX
    places = jnp.stack(
        [(x + step) % NX * depth for step in range(NX)] + [(x + 2) % NX * depth + depth // 2]
    ).astype(jnp.int32)

    cut = depth // 2
    starts = group_places(group_date, group)

    raw = pick(states, 0, wa, 1)
    raw_left = lax.ppermute(raw, AXES, X_UP)
    raw_right = lax.ppermute(raw, AXES, X_DOWN)
    raw_far = lax.ppermute(raw, AXES, X_FAR)
    pair = lax.ppermute(increments, AXES, Z_PAIR)
    sentb = pick(states, wa, wb, 2)
    gotc = exchange(pick(states, wa + wb, wc, 2)).reshape(-1, wc)

    sentb, raw, raw_left, raw_right, raw_far, gotc, increments, pair = barrier(
        (sentb, raw, raw_left, raw_right, raw_far, gotc, increments, pair)
    )
    left = lax.ppermute(gotc, AXES, X_UP)
    right = lax.ppermute(gotc, AXES, X_DOWN)
    near = jnp.stack([increments, pair])
    below = lax.ppermute(near, AXES, Y_UP)
    above = lax.ppermute(near, AXES, Y_DOWN)
    across = lax.ppermute(near, AXES, Y_FAR)
    gotb = exchange(sentb).reshape(-1, wb)
    senta = join([raw, raw_right, raw_far, raw_left])

    senta, gotb, gotc, left, right, to_right, to_left = barrier(
        (senta, gotb, gotc, left, right, left[:cut], right[cut:])
    )
    far_left = lax.ppermute(to_right, AXES, X_UP)
    far_right = lax.ppermute(to_left, AXES, X_DOWN)
    left_b = lax.ppermute(gotb, AXES, X_UP)
    right_b = lax.ppermute(gotb, AXES, X_DOWN)
    mine = jnp.stack([near, above, across, below]).reshape(dates // 2, -1)
    other = lax.ppermute(mine, AXES, CORE)
    gota = exchange(senta).reshape(2 * NCOL, NX, group, wa)
    rows, inc_sum = align(starts, mine, other)
    ring = [gotc, right, left, far_left, far_right]
    out = product(ring_panel, places, rows, inc_sum, ring, wa + wb, columns, None)

    left_b, right_b, out = barrier((left_b, right_b, out))
    far_left_b = lax.ppermute(left_b[:cut], AXES, X_UP)
    far_right_b = lax.ppermute(right_b[cut:], AXES, X_DOWN)
    out = product(exchange_panel, places, rows, inc_sum, [gota], 0, columns, out)
    ring = [gotb, right_b, left_b, far_left_b, far_right_b]
    return product(ring_panel, places, rows, inc_sum, ring, wa, columns, out)


def solution(mesh):
    in_specs = (P("col", "row"), P(("row", "col"), None), P())
    out_specs = P("row", "col")
    return jax.shard_map(body, mesh=mesh, in_specs=in_specs, out_specs=out_specs, check_vma=False)
```

```python
import functools

import jax
import jax.numpy as jnp
from jax import lax
from jax.experimental import pallas as pl
from jax.experimental.pallas import tpu as pltpu
from jax.sharding import PartitionSpec as P

AXES = ("row", "col")
NX, NY, NZ, NC = 4, 4, 4, 2
NCOL = NY * 2 * NC
TILE = 512
BLOCK = 256
WEIGHT = 6
WIDTHS = (1024, 1536, 1536)


def device(x, y, z, c):
    return ((x % NX) * 2 + (z % NZ) // 2) * NCOL + ((y % NY) * 2 + (z % NZ) % 2) * NC + c


def moves(to):
    return [
        (device(x, y, z, c), device(*to(x, y, z, c)))
        for x in range(NX) for y in range(NY) for z in range(NZ) for c in range(NC)
    ]


X_UP = moves(lambda x, y, z, c: (x + 1, y, z, c))
X_DOWN = moves(lambda x, y, z, c: (x - 1, y, z, c))
X_FAR = moves(lambda x, y, z, c: (x + 2, y, z, c))
Y_UP = moves(lambda x, y, z, c: (x, y + 1, z, c))
Y_DOWN = moves(lambda x, y, z, c: (x, y - 1, z, c))
Y_FAR = moves(lambda x, y, z, c: (x, y + 2, z, c))
Z_PAIR = moves(lambda x, y, z, c: (x, y, z ^ 1, c))
CORE = moves(lambda x, y, z, c: (x, y, z, 1 - c))
SAME_X = [[x * 2 * NCOL + i for i in range(2 * NCOL)] for x in range(NX)]


def copy_all(copies, sems):
    started = [pltpu.make_async_copy(a, b, sems.at[i]) for i, (a, b) in enumerate(copies)]
    for copy in started:
        copy.start()
    for copy in started:
        copy.wait()


def repeat(held, out_ref, sems):
    targets = held.shape[0]
    times = out_ref.shape[0] // targets
    copy_all([(held, out_ref.at[pl.ds(i * targets, targets)]) for i in range(times)], sems)


def pick_kernel(offset, states_ref, out_ref, held, sems):
    targets, _, width = held.shape
    columns = states_ref.shape[1] // targets
    copy_all(
        [
            (states_ref.at[:, pl.ds(t * columns + offset, width)], held.at[t])
            for t in range(targets)
        ],
        sems,
    )
    repeat(held, out_ref, sems)


def pick(states, offset, width, times):
    shape = (NCOL, states.shape[0], width)
    return pl.pallas_call(
        functools.partial(pick_kernel, offset),
        out_shape=jax.ShapeDtypeStruct((times * NCOL,) + shape[1:], states.dtype),
        in_specs=[pl.BlockSpec(memory_space=pl.ANY)],
        out_specs=pl.BlockSpec(memory_space=pl.ANY),
        scratch_shapes=[pltpu.VMEM(shape, states.dtype), pltpu.SemaphoreType.DMA((NCOL,))],
        compiler_params=pltpu.CompilerParams(vmem_limit_bytes=60 * 2**20),
        cost_estimate=pl.CostEstimate(flops=width, bytes_accessed=width, transcendentals=0),
        name="pick",
    )(states)


def join_kernel(*refs):
    parts, out_ref, held, sems = refs[:-3], refs[-3], refs[-2], refs[-1]
    copy_all([(part, held.at[:, i]) for i, part in enumerate(parts)], sems)
    repeat(held, out_ref, sems)


def join(parts):
    targets, group, width = parts[0].shape
    shape = (targets, len(parts), group, width)
    return pl.pallas_call(
        join_kernel,
        out_shape=jax.ShapeDtypeStruct((2 * targets,) + shape[1:], parts[0].dtype),
        in_specs=[pl.BlockSpec(memory_space=pl.ANY)] * len(parts),
        out_specs=pl.BlockSpec(memory_space=pl.ANY),
        scratch_shapes=[
            pltpu.VMEM(shape, parts[0].dtype),
            pltpu.SemaphoreType.DMA((len(parts),)),
        ],
        compiler_params=pltpu.CompilerParams(vmem_limit_bytes=60 * 2**20),
        cost_estimate=pl.CostEstimate(flops=width, bytes_accessed=width, transcendentals=0),
        name="join",
    )(*parts)


def align_kernel(starts, mine_ref, other_ref, out_ref, sum_ref, held, sem):
    dates, comps = held.shape
    group = dates // starts.shape[0]
    half = dates // 2

    def send(i, carry):
        start = starts[i]
        target = held.at[pl.ds(pl.multiple_of(i * group, group), group)]

        @pl.when(start < half)
        def _():
            source = mine_ref.at[pl.ds(pl.multiple_of(start, group), group)]
            pltpu.make_async_copy(source, target, sem).start()

        @pl.when(start >= half)
        def _():
            source = other_ref.at[pl.ds(pl.multiple_of(start - half, group), group)]
            pltpu.make_async_copy(source, target, sem).start()

        return carry

    lax.fori_loop(0, starts.shape[0], send, 0)
    pltpu.make_async_copy(held, held, sem).wait()
    step = 256
    total = jnp.zeros((comps, 1), jnp.float32)
    for i in range(dates // step):
        turned = held[i * step:(i + 1) * step, :].T
        out_ref[:, i * step:(i + 1) * step] = turned
        total = total + jnp.sum(turned.astype(jnp.float32), axis=1, keepdims=True)
    sum_ref[...] = total


def align(starts, mine, other):
    dates, comps = 2 * mine.shape[0], mine.shape[1]
    return pl.pallas_call(
        align_kernel,
        out_shape=(
            jax.ShapeDtypeStruct((comps, dates), mine.dtype),
            jax.ShapeDtypeStruct((comps, 1), jnp.float32),
        ),
        in_specs=[
            pl.BlockSpec(memory_space=pltpu.SMEM),
            pl.BlockSpec(memory_space=pl.ANY),
            pl.BlockSpec(memory_space=pl.ANY),
        ],
        out_specs=(
            pl.BlockSpec(memory_space=pltpu.VMEM),
            pl.BlockSpec(memory_space=pltpu.VMEM),
        ),
        scratch_shapes=[pltpu.VMEM((dates, comps), mine.dtype), pltpu.SemaphoreType.DMA],
        compiler_params=pltpu.CompilerParams(vmem_limit_bytes=60 * 2**20),
        cost_estimate=pl.CostEstimate(flops=comps, bytes_accessed=comps, transcendentals=0),
        name="align",
    )(starts, mine, other)


def exchange_panel(places, panels):
    sources, nx, group, width = panels[0].shape
    depth = sources * group
    return [
        (pl.multiple_of(places[i], depth), panels[0][:, i].reshape(depth, width))
        for i in range(nx)
    ]


def ring_panel(places, panels):
    order = (0, 1, 3, 2, 4)
    return [
        (pl.multiple_of(places[i], panel.shape[0]), panel[...]) for i, panel in zip(order, panels)
    ]


def product_kernel(pieces, places, rows_ref, sum_ref, *refs):
    comps, dates = rows_ref.shape
    panels, out_ref = refs[:-1], refs[-1]
    parts = pieces(places, panels)
    state_sum = sum(jnp.sum(part.astype(jnp.float32), axis=0, keepdims=True) for _, part in parts)
    state_mean = state_sum / dates
    for start in range(0, comps, BLOCK):
        block = pl.ds(start, BLOCK)
        acc = sum(
            jnp.dot(
                rows_ref[block, pl.ds(place, part.shape[0])],
                part,
                preferred_element_type=jnp.float32,
            )
            for place, part in parts
        )
        inc_mean = sum_ref[block, :] / dates
        out_ref[block, :] = (acc - dates * (inc_mean * state_mean)) * (1.0 / (dates - 1))


def product(pieces, places, rows, inc_sum, panels, offset, columns, out):
    comps, dates = rows.shape
    width = panels[0].shape[-1]
    tile = TILE if width % TILE == 0 and offset % TILE == 0 else TILE // 2
    base = offset // tile
    whole = pl.Buffered(1)
    in_specs = [
        pl.BlockSpec(memory_space=pltpu.SMEM),
        pl.BlockSpec(rows.shape, lambda j: (0, 0), pipeline_mode=whole),
        pl.BlockSpec(inc_sum.shape, lambda j: (0, 0), pipeline_mode=whole),
    ]
    for panel in panels:
        lead = (0,) * (panel.ndim - 1)
        in_specs.append(pl.BlockSpec(panel.shape[:-1] + (tile,), lambda j, lead=lead: lead + (j,)))
    args = [places, rows, inc_sum] + panels
    aliases = {}
    kernel = functools.partial(product_kernel, pieces)
    if out is not None:
        in_specs.append(pl.BlockSpec(memory_space=pl.ANY))
        aliases = {len(args): 0}
        args.append(out)

        def kernel(*refs):
            product_kernel(pieces, *refs[:-2], refs[-1])

    return pl.pallas_call(
        kernel,
        out_shape=jax.ShapeDtypeStruct((comps, columns), jnp.float32),
        grid=(width // tile,),
        in_specs=in_specs,
        out_specs=pl.BlockSpec((comps, tile), lambda j: (0, base + j)),
        input_output_aliases=aliases,
        compiler_params=pltpu.CompilerParams(vmem_limit_bytes=60 * 2**20),
        cost_estimate=pl.CostEstimate(
            flops=2 * comps * dates * width * WEIGHT,
            bytes_accessed=(2 * comps * dates + 2 * dates * width + 4 * comps * width) * WEIGHT,
            transcendentals=0,
        ),
        name="product",
    )(*args)


def group_places(group_date, group):
    per = group_date.shape[0] // NCOL
    col = lax.axis_index("col")
    y, zl, c = col // (2 * NC), (col // NC) % 2, col % NC
    owner = group_date // per
    oy, oz, oc = owner // (2 * NC), (owner // NC) % 2, owner % NC
    place = ((((oc + c) % 2) * NY + (oy - y + NY) % NY) * 2 + (oz + zl) % 2) * per + group_date % per
    return (place * group).astype(jnp.int32)


def body(increments, states, group_date):
    group, total = states.shape
    columns = total // NCOL
    dates = group * group_date.shape[0]
    barrier = lax.optimization_barrier

    def exchange(sent):
        return lax.all_to_all(sent, AXES, 0, 0, tiled=True, axis_index_groups=SAME_X)

    wa, wb, wc = WIDTHS
    x = lax.axis_index("row") // 2
    depth = dates // NX
    places = jnp.stack(
        [(x + step) % NX * depth for step in range(NX)] + [(x + 2) % NX * depth + depth // 2]
    ).astype(jnp.int32)

    cut = depth // 2
    starts = group_places(group_date, group)

    raw = pick(states, 0, wa, 1)
    raw_left = lax.ppermute(raw, AXES, X_UP)
    raw_right = lax.ppermute(raw, AXES, X_DOWN)
    raw_far = lax.ppermute(raw, AXES, X_FAR)
    pair = lax.ppermute(increments, AXES, Z_PAIR)
    sentb = pick(states, wa, wb, 2)
    gotc = exchange(pick(states, wa + wb, wc, 2)).reshape(-1, wc)

    sentb, raw, raw_left, raw_right, raw_far, gotc, increments, pair = barrier(
        (sentb, raw, raw_left, raw_right, raw_far, gotc, increments, pair)
    )
    left = lax.ppermute(gotc, AXES, X_UP)
    right = lax.ppermute(gotc, AXES, X_DOWN)
    near = jnp.stack([increments, pair])
    below = lax.ppermute(near, AXES, Y_UP)
    above = lax.ppermute(near, AXES, Y_DOWN)
    across = lax.ppermute(near, AXES, Y_FAR)
    gotb = exchange(sentb).reshape(-1, wb)
    senta = join([raw, raw_right, raw_far, raw_left])

    senta, gotb, gotc, left, right, to_right, to_left = barrier(
        (senta, gotb, gotc, left, right, left[:cut], right[cut:])
    )
    far_left = lax.ppermute(to_right, AXES, X_UP)
    far_right = lax.ppermute(to_left, AXES, X_DOWN)
    left_b = lax.ppermute(gotb, AXES, X_UP)
    right_b = lax.ppermute(gotb, AXES, X_DOWN)
    mine = jnp.stack([near, above, across, below]).reshape(dates // 2, -1)
    other = lax.ppermute(mine, AXES, CORE)
    gota = exchange(senta).reshape(2 * NCOL, NX, group, wa)
    rows, inc_sum = align(starts, mine, other)
    ring = [gotc, right, left, far_left, far_right]
    out = product(ring_panel, places, rows, inc_sum, ring, wa + wb, columns, None)

    left_b, right_b, out = barrier((left_b, right_b, out))
    far_left_b = lax.ppermute(left_b[:cut], AXES, X_UP)
    far_right_b = lax.ppermute(right_b[cut:], AXES, X_DOWN)
    out = product(exchange_panel, places, rows, inc_sum, [gota], 0, columns, out)
    ring = [gotb, right_b, left_b, far_left_b, far_right_b]
    return product(ring_panel, places, rows, inc_sum, ring, wa, columns, out)


def solution(mesh):
    in_specs = (P("col", "row"), P(("row", "col"), None), P())
    out_specs = P("row", "col")
    return jax.shard_map(body, mesh=mesh, in_specs=in_specs, out_specs=out_specs, check_vma=False)
```

```python
import functools

import jax
import jax.numpy as jnp
from jax import lax
from jax.experimental import pallas as pl
from jax.experimental.pallas import tpu as pltpu
from jax.sharding import PartitionSpec as P

AXES = ("row", "col")
NX, NY, NZ, NC = 4, 4, 4, 2
NCOL = NY * 2 * NC
TILE = 256
BLOCK = 256
WEIGHT = 6
WIDTHS = (1024, 1536, 1536)


def device(x, y, z, c):
    return ((x % NX) * 2 + (z % NZ) // 2) * NCOL + ((y % NY) * 2 + (z % NZ) % 2) * NC + c


def moves(to):
    return [
        (device(x, y, z, c), device(*to(x, y, z, c)))
        for x in range(NX) for y in range(NY) for z in range(NZ) for c in range(NC)
    ]


X_UP = moves(lambda x, y, z, c: (x + 1, y, z, c))
X_DOWN = moves(lambda x, y, z, c: (x - 1, y, z, c))
X_FAR = moves(lambda x, y, z, c: (x + 2, y, z, c))
Y_UP = moves(lambda x, y, z, c: (x, y + 1, z, c))
Y_DOWN = moves(lambda x, y, z, c: (x, y - 1, z, c))
Y_FAR = moves(lambda x, y, z, c: (x, y + 2, z, c))
Z_PAIR = moves(lambda x, y, z, c: (x, y, z ^ 1, c))
CORE = moves(lambda x, y, z, c: (x, y, z, 1 - c))
SAME_X = [[x * 2 * NCOL + i for i in range(2 * NCOL)] for x in range(NX)]


def copy_all(copies, sems):
    started = [pltpu.make_async_copy(a, b, sems.at[i]) for i, (a, b) in enumerate(copies)]
    for copy in started:
        copy.start()
    for copy in started:
        copy.wait()


def repeat(held, out_ref, sems):
    targets = held.shape[0]
    times = out_ref.shape[0] // targets
    copy_all([(held, out_ref.at[pl.ds(i * targets, targets)]) for i in range(times)], sems)


def pick_kernel(offset, states_ref, out_ref, held, sems):
    targets, _, width = held.shape
    columns = states_ref.shape[1] // targets
    copy_all(
        [
            (states_ref.at[:, pl.ds(t * columns + offset, width)], held.at[t])
            for t in range(targets)
        ],
        sems,
    )
    repeat(held, out_ref, sems)


def pick(states, offset, width, times):
    shape = (NCOL, states.shape[0], width)
    return pl.pallas_call(
        functools.partial(pick_kernel, offset),
        out_shape=jax.ShapeDtypeStruct((times * NCOL,) + shape[1:], states.dtype),
        in_specs=[pl.BlockSpec(memory_space=pl.ANY)],
        out_specs=pl.BlockSpec(memory_space=pl.ANY),
        scratch_shapes=[pltpu.VMEM(shape, states.dtype), pltpu.SemaphoreType.DMA((NCOL,))],
        compiler_params=pltpu.CompilerParams(vmem_limit_bytes=60 * 2**20),
        cost_estimate=pl.CostEstimate(flops=width, bytes_accessed=width, transcendentals=0),
        name="pick",
    )(states)


def join_kernel(*refs):
    parts, out_ref, held, sems = refs[:-3], refs[-3], refs[-2], refs[-1]
    copy_all([(part, held.at[:, i]) for i, part in enumerate(parts)], sems)
    repeat(held, out_ref, sems)


def join(parts):
    targets, group, width = parts[0].shape
    shape = (targets, len(parts), group, width)
    return pl.pallas_call(
        join_kernel,
        out_shape=jax.ShapeDtypeStruct((2 * targets,) + shape[1:], parts[0].dtype),
        in_specs=[pl.BlockSpec(memory_space=pl.ANY)] * len(parts),
        out_specs=pl.BlockSpec(memory_space=pl.ANY),
        scratch_shapes=[
            pltpu.VMEM(shape, parts[0].dtype),
            pltpu.SemaphoreType.DMA((len(parts),)),
        ],
        compiler_params=pltpu.CompilerParams(vmem_limit_bytes=60 * 2**20),
        cost_estimate=pl.CostEstimate(flops=width, bytes_accessed=width, transcendentals=0),
        name="join",
    )(*parts)


def align_kernel(starts, mine_ref, other_ref, out_ref, sum_ref, held, sem):
    dates, comps = held.shape
    group = dates // starts.shape[0]
    half = dates // 2

    def send(i, carry):
        start = starts[i]
        target = held.at[pl.ds(pl.multiple_of(i * group, group), group)]

        @pl.when(start < half)
        def _():
            source = mine_ref.at[pl.ds(pl.multiple_of(start, group), group)]
            pltpu.make_async_copy(source, target, sem).start()

        @pl.when(start >= half)
        def _():
            source = other_ref.at[pl.ds(pl.multiple_of(start - half, group), group)]
            pltpu.make_async_copy(source, target, sem).start()

        return carry

    lax.fori_loop(0, starts.shape[0], send, 0)
    pltpu.make_async_copy(held, held, sem).wait()
    step = 256
    total = jnp.zeros((comps, 1), jnp.float32)
    for i in range(dates // step):
        turned = held[i * step:(i + 1) * step, :].T
        out_ref[:, i * step:(i + 1) * step] = turned
        total = total + jnp.sum(turned.astype(jnp.float32), axis=1, keepdims=True)
    sum_ref[...] = total


def align(starts, mine, other):
    dates, comps = 2 * mine.shape[0], mine.shape[1]
    return pl.pallas_call(
        align_kernel,
        out_shape=(
            jax.ShapeDtypeStruct((comps, dates), mine.dtype),
            jax.ShapeDtypeStruct((comps, 1), jnp.float32),
        ),
        in_specs=[
            pl.BlockSpec(memory_space=pltpu.SMEM),
            pl.BlockSpec(memory_space=pl.ANY),
            pl.BlockSpec(memory_space=pl.ANY),
        ],
        out_specs=(
            pl.BlockSpec(memory_space=pltpu.VMEM),
            pl.BlockSpec(memory_space=pltpu.VMEM),
        ),
        scratch_shapes=[pltpu.VMEM((dates, comps), mine.dtype), pltpu.SemaphoreType.DMA],
        compiler_params=pltpu.CompilerParams(vmem_limit_bytes=60 * 2**20),
        cost_estimate=pl.CostEstimate(flops=comps, bytes_accessed=comps, transcendentals=0),
        name="align",
    )(starts, mine, other)


def exchange_panel(places, panels):
    sources, nx, group, width = panels[0].shape
    depth = sources * group
    return [
        (pl.multiple_of(places[i], depth), panels[0][:, i].reshape(depth, width))
        for i in range(nx)
    ]


def ring_panel(places, panels):
    order = (0, 1, 3, 2, 4)
    return [
        (pl.multiple_of(places[i], panel.shape[0]), panel[...]) for i, panel in zip(order, panels)
    ]


def product_kernel(pieces, places, rows_ref, sum_ref, *refs):
    comps, dates = rows_ref.shape
    panels, out_ref = refs[:-1], refs[-1]
    parts = pieces(places, panels)
    state_sum = sum(jnp.sum(part.astype(jnp.float32), axis=0, keepdims=True) for _, part in parts)
    state_mean = state_sum / dates
    for start in range(0, comps, BLOCK):
        block = pl.ds(start, BLOCK)
        acc = sum(
            jnp.dot(
                rows_ref[block, pl.ds(place, part.shape[0])],
                part,
                preferred_element_type=jnp.float32,
            )
            for place, part in parts
        )
        inc_mean = sum_ref[block, :] / dates
        out_ref[block, :] = (acc - dates * (inc_mean * state_mean)) * (1.0 / (dates - 1))


def product(pieces, places, rows, inc_sum, panels, offset, columns, out):
    comps, dates = rows.shape
    width = panels[0].shape[-1]
    tile = TILE if width % TILE == 0 and offset % TILE == 0 else TILE // 2
    base = offset // tile
    whole = pl.Buffered(1)
    in_specs = [
        pl.BlockSpec(memory_space=pltpu.SMEM),
        pl.BlockSpec(rows.shape, lambda j: (0, 0), pipeline_mode=whole),
        pl.BlockSpec(inc_sum.shape, lambda j: (0, 0), pipeline_mode=whole),
    ]
    for panel in panels:
        lead = (0,) * (panel.ndim - 1)
        in_specs.append(pl.BlockSpec(panel.shape[:-1] + (tile,), lambda j, lead=lead: lead + (j,)))
    args = [places, rows, inc_sum] + panels
    aliases = {}
    kernel = functools.partial(product_kernel, pieces)
    if out is not None:
        in_specs.append(pl.BlockSpec(memory_space=pl.ANY))
        aliases = {len(args): 0}
        args.append(out)

        def kernel(*refs):
            product_kernel(pieces, *refs[:-2], refs[-1])

    return pl.pallas_call(
        kernel,
        out_shape=jax.ShapeDtypeStruct((comps, columns), jnp.float32),
        grid=(width // tile,),
        in_specs=in_specs,
        out_specs=pl.BlockSpec((comps, tile), lambda j: (0, base + j)),
        input_output_aliases=aliases,
        compiler_params=pltpu.CompilerParams(vmem_limit_bytes=60 * 2**20),
        cost_estimate=pl.CostEstimate(
            flops=2 * comps * dates * width * WEIGHT,
            bytes_accessed=(2 * comps * dates + 2 * dates * width + 4 * comps * width) * WEIGHT,
            transcendentals=0,
        ),
        name="product",
    )(*args)


def group_places(group_date, group):
    per = group_date.shape[0] // NCOL
    col = lax.axis_index("col")
    y, zl, c = col // (2 * NC), (col // NC) % 2, col % NC
    owner = group_date // per
    oy, oz, oc = owner // (2 * NC), (owner // NC) % 2, owner % NC
    place = ((((oc + c) % 2) * NY + (oy - y + NY) % NY) * 2 + (oz + zl) % 2) * per + group_date % per
    return (place * group).astype(jnp.int32)


def body(increments, states, group_date):
    group, total = states.shape
    columns = total // NCOL
    dates = group * group_date.shape[0]
    barrier = lax.optimization_barrier

    def exchange(sent):
        return lax.all_to_all(sent, AXES, 0, 0, tiled=True, axis_index_groups=SAME_X)

    wa, wb, wc = WIDTHS
    x = lax.axis_index("row") // 2
    depth = dates // NX
    places = jnp.stack(
        [(x + step) % NX * depth for step in range(NX)] + [(x + 2) % NX * depth + depth // 2]
    ).astype(jnp.int32)

    cut = depth // 2
    starts = group_places(group_date, group)

    raw = pick(states, 0, wa, 1)
    raw_left = lax.ppermute(raw, AXES, X_UP)
    raw_right = lax.ppermute(raw, AXES, X_DOWN)
    raw_far = lax.ppermute(raw, AXES, X_FAR)
    pair = lax.ppermute(increments, AXES, Z_PAIR)
    sentb = pick(states, wa, wb, 2)
    gotc = exchange(pick(states, wa + wb, wc, 2)).reshape(-1, wc)

    sentb, raw, raw_left, raw_right, raw_far, gotc, increments, pair = barrier(
        (sentb, raw, raw_left, raw_right, raw_far, gotc, increments, pair)
    )
    left = lax.ppermute(gotc, AXES, X_UP)
    right = lax.ppermute(gotc, AXES, X_DOWN)
    near = jnp.stack([increments, pair])
    below = lax.ppermute(near, AXES, Y_UP)
    above = lax.ppermute(near, AXES, Y_DOWN)
    across = lax.ppermute(near, AXES, Y_FAR)
    gotb = exchange(sentb).reshape(-1, wb)
    senta = join([raw, raw_right, raw_far, raw_left])

    senta, gotb, gotc, left, right, to_right, to_left = barrier(
        (senta, gotb, gotc, left, right, left[:cut], right[cut:])
    )
    far_left = lax.ppermute(to_right, AXES, X_UP)
    far_right = lax.ppermute(to_left, AXES, X_DOWN)
    left_b = lax.ppermute(gotb, AXES, X_UP)
    right_b = lax.ppermute(gotb, AXES, X_DOWN)
    mine = jnp.stack([near, above, across, below]).reshape(dates // 2, -1)
    other = lax.ppermute(mine, AXES, CORE)
    gota = exchange(senta).reshape(2 * NCOL, NX, group, wa)
    rows, inc_sum = align(starts, mine, other)
    ring = [gotc, right, left, far_left, far_right]
    out = product(ring_panel, places, rows, inc_sum, ring, wa + wb, columns, None)

    left_b, right_b, out = barrier((left_b, right_b, out))
    far_left_b = lax.ppermute(left_b[:cut], AXES, X_UP)
    far_right_b = lax.ppermute(right_b[cut:], AXES, X_DOWN)
    out = product(exchange_panel, places, rows, inc_sum, [gota], 0, columns, out)
    ring = [gotb, right_b, left_b, far_left_b, far_right_b]
    return product(ring_panel, places, rows, inc_sum, ring, wa, columns, out)


def solution(mesh):
    in_specs = (P("col", "row"), P(("row", "col"), None), P())
    out_specs = P("row", "col")
    return jax.shard_map(body, mesh=mesh, in_specs=in_specs, out_specs=out_specs, check_vma=False)
```
